32 devices in a mesh: grp: 2 (over y), blk: 8 (over z, x), sub: 2 (over core).
Axes of the slice: x: 2, y: 2, z: 4, core: 2. Of those that a mesh axis runs over, the one named last changes fastest.
Arguments:
- log_rate: float32 [16384], P(('grp', 'blk')), parts along dimension 0, may hold values from -1 to 0.5
- log_state: float32 [16384], P(('grp', 'blk')), parts along dimension 0, may hold values from -1 to 1
- load: float32 [16384], P(('grp', 'blk')), parts along dimension 0, may hold values from 1 to 4
- a_sigma: float32 [16384], P(('grp', 'blk')), parts along dimension 0, may hold values from 0.5 to 2
- b_sigma: float32 [16384], P(('grp', 'blk')), parts along dimension 0, may hold values from 0.5 to 2
- log_dc: float32 [16384], P(('grp', 'blk')), parts along dimension 0, may hold values from -0.5 to 0.5
- near_field: float32 [64, 128, 128], P(('blk', 'sub')), may hold values from -0.25 to 2.5, as said below
- col_cluster: int32 [8, 2, 88], P(None, 'sub'), may hold values from 0 to 63, as said below
- row_cluster: int32 [8, 2, 88], P(None, 'sub'), may hold values from 0 to 63, as said below
- ranks: int32 [8, 2, 88], P('blk', 'sub'), may hold values from 6 to 48
- col_factor: float32 [8, 2, 88, 48, 128], P('blk', 'sub'), may hold values from -0.5 to 0.5
- row_factor: float32 [8, 2, 88, 48, 128], P('blk', 'sub'), may hold values from -0.24 to 0.24
Outputs:
- new_log_rate: float32 [16384], P(('grp', 'blk')), parts along dimension 0
- new_log_state: float32 [16384], P(('grp', 'blk')), parts along dimension 0
The draws below stay inside these ranges and needn't reach their ends.
There are 2 independent parts, one for each index of `grp`. The reference program is written for one: setup_inputs(seed, part) draws one part's arguments, and reference() takes and returns one part's arrays. A program takes and returns all parts, laid end to end along the dimension named above; an argument that names none is the same for every part. Nothing has to cross between parts.
Inputs may be any that keep to these rules, and one draw needn't show every extreme that they name: `col_cluster`: cluster c holds elements c * 128 to c * 128 + 127 and lies on blk device c // 8. For every owner o and group s, at most 22 of the 88 blocks take their columns from clusters of one device, and exactly 22 from some device. `row_cluster`: for every owner o and group s, at most 22 of the 88 blocks write to row clusters of one device, and exactly 22 to some device. `near_field`: each diagonal entry is 1 or more, and the other entries of a row are small beside it.
All inputs are finite; a program needn't handle non-finite values.
Results may differ from the reference program's by a relative error of at most 0.0003.
Values sent between devices are 32-bit elements; how exact they have to be, the bound alone decides.
No kernel may reach another device: no remote copies, remote signals or barrier semaphores. Data moves between devices by JAX's collectives and lax.ppermute only.
A program may use at most 64 MiB of HBM per device.

```python
import math
import jax
import jax.numpy as jnp
from jax import lax

CL = 128
CPD = 8
NB = 88
KMAX = 48
OWNERS = 8
SUBS = 2
CLUSTERS = 64
ELEMENTS = 8192
CAP = 22


def route_table(key):
    all_keys = jax.random.split(key, OWNERS * SUBS)
    tickets = OWNERS * CAP
    source = jnp.arange(tickets, dtype=jnp.int32) // CAP

    def single_table(sub_key):
        key_ranking, key_heavy, key_shuffle, key_cluster = jax.random.split(sub_key, 4)
        scores = jax.random.permutation(key_ranking, tickets).astype(jnp.int32)
        heavy_source = jax.random.randint(key_heavy, (), 0, OWNERS).astype(jnp.int32)
        scores = jnp.where(source == heavy_source, scores - tickets, scores)
        ranking = jnp.argsort(scores, stable=True)
        chosen = source[ranking[:NB]]
        chosen = chosen[jax.random.permutation(key_shuffle, NB)]
        within = jax.random.randint(key_cluster, (NB,), 0, CPD).astype(jnp.int32)
        return (chosen * CPD + within).astype(jnp.int32)
    return jax.vmap(single_table)(all_keys).reshape(OWNERS, SUBS, NB)


def draw_col_cluster(key, part):
    key = jax.random.fold_in(key, 11)
    return route_table(key)


def draw_row_cluster(key, part):
    key = jax.random.fold_in(key, 23)
    return route_table(key)


def draw_near_field(key, part):
    key = jax.random.fold_in(key, 5)
    key_coupling, key_diagonal = jax.random.split(key)
    coupling = jnp.clip(jax.random.normal(key_coupling, (CLUSTERS, CL, CL), jnp.float32), -5.0, 5.0) * (0.5 * CL ** (-0.5))
    diagonal_values = jax.random.uniform(key_diagonal, (CLUSTERS, CL), jnp.float32, 1.0, 2.0)
    on_diagonal = jnp.eye(CL, dtype=bool)[None, :, :]
    coupling = jnp.clip(coupling, -0.25, 0.25)
    return jnp.where(on_diagonal, diagonal_values[:, :, None], coupling).astype(jnp.float32)


def with_ends(values, own_key, least, largest):
    shape = values.shape
    place = [jax.random.randint(jax.random.fold_in(own_key, axis), (), 0, shape[axis]) for axis in range(len(shape))]
    values = values.at[tuple(place)].set(least)
    longest = shape.index(max(shape))
    place[longest] = (place[longest] + 1) % shape[longest]
    return values.at[tuple(place)].set(largest)


def steps_of(rng, dims, cuts, low, high):
    def one(axis_at, parts):
        steps = jax.random.uniform(jax.random.fold_in(jax.random.fold_in(rng, 6), axis_at), (parts,), jnp.float32, low / len(cuts), high / len(cuts))
        return jnp.repeat(jnp.exp(steps), dims[axis_at] // parts).reshape((-1,) + (1,) * (len(dims) - axis_at - 1))

    factor_of = one(*cuts[0])
    for cut in cuts[1:]:
        factor_of = factor_of * one(*cut)
    return factor_of


def bell_draw(own_key, extent, width, reach, cuts=(), kind=jnp.bfloat16):
    values = jax.random.normal(own_key, extent, jnp.float32) * width
    if len(cuts) > 0:
        values = steps_of(own_key, extent, cuts, -0.22, 0.18) * values
    return jnp.clip(values, min=-reach, max=reach).astype(kind)


def setup_inputs(seed: int = 0, part: int = 0) -> dict:
    keys = jax.random.split(jax.random.key(seed), 13)
    part_splits = jax.random.split(jax.random.fold_in(keys[12], part), 13)
    return {
        "log_rate": jnp.clip(-1.0 + 1.5 * jax.random.uniform(part_splits[0], (ELEMENTS,), jnp.float32) ** steps_of(part_splits[0], (ELEMENTS,), ((0, 8),), -0.2, 0.2), -1.0, 0.5),
        "log_state": jnp.clip(jax.random.uniform(part_splits[1], (ELEMENTS,), jnp.float32, -1.0, 1.0) * steps_of(part_splits[1], (ELEMENTS,), ((0, 8),), -0.4, 0.0), -1.0, 1.0),
        "load": jnp.clip(1.0 + 3.0 * jax.random.uniform(part_splits[2], (ELEMENTS,), jnp.float32) ** steps_of(part_splits[2], (ELEMENTS,), ((0, 8),), -0.2, 0.2), 1.0, 4.0),
        "a_sigma": jnp.clip(jnp.exp(math.log(2.0) - 1.3862944 * jax.random.uniform(part_splits[3], (ELEMENTS,), jnp.float32) ** steps_of(part_splits[3], (ELEMENTS,), ((0, 8),), -0.2, 0.2)), 0.5, 2.0),
        "b_sigma": jnp.clip(0.5 + 1.5 * jax.random.uniform(part_splits[4], (ELEMENTS,), jnp.float32) ** steps_of(part_splits[4], (ELEMENTS,), ((0, 8),), -0.2, 0.2), 0.5, 2.0),
        "log_dc": jnp.clip(jax.random.uniform(part_splits[5], (ELEMENTS,), jnp.float32, -0.5, 0.5) * steps_of(part_splits[5], (ELEMENTS,), ((0, 8),), -0.4, 0.0), -0.5, 0.5),
        "near_field": draw_near_field(jax.random.fold_in(keys[12], 71), part),
        "col_cluster": draw_col_cluster(jax.random.fold_in(keys[12], 71), part),
        "row_cluster": draw_row_cluster(jax.random.fold_in(keys[12], 71), part),
        "ranks": with_ends(jax.random.randint(keys[9], (OWNERS, SUBS, NB), KMAX // 8, KMAX + 1), jax.random.fold_in(keys[9], 1), KMAX // 8, KMAX).astype(jnp.int32),
        "col_factor": bell_draw(keys[10], (OWNERS, SUBS, NB, KMAX, CL), CL ** -0.5, 0.5, ((0, 8), (1, 2)), jnp.float32),
        "row_factor": bell_draw(keys[11], (OWNERS, SUBS, NB, KMAX, CL), 0.04, 0.24, ((0, 8), (1, 2)), jnp.float32),
    }


precise = lax.Precision.HIGHEST
damping = 0.5
time_step = 0.25


def fault_rates(log_values, log_states, traction, load, a_sigma, b_sigma, log_dc):
    state_rate = jnp.exp(-log_states) - jnp.exp(log_values - log_dc)
    rate_rate = (load - traction - b_sigma * state_rate) / (a_sigma + damping * jnp.exp(log_values))
    return rate_rate, state_rate


def reference(log_rate, log_state, load, a_sigma, b_sigma, log_dc, near_field, col_cluster, row_cluster, ranks, col_factor, row_factor):
    levels = jnp.arange(KMAX, dtype=jnp.int32)

    def traction_of(log_values):
        slip_rate = jnp.exp(log_values).reshape(CLUSTERS, CL)
        near_part = jnp.einsum("cij,cj->ci", near_field, slip_rate, precision=precise)

        def owner_step(summed, pieces):
            col_ids, row_ids, rank_row, column_factor, row_local = pieces
            block_input = slip_rate[col_ids]
            coefficient = jnp.einsum("sbkl,sbl->sbk", column_factor, block_input, precision=precise)
            coefficient = jnp.where(levels[None, None, :] < rank_row[:, :, None], coefficient, jnp.float32(0.0))
            block_output = jnp.einsum("sbkl,sbk->sbl", row_local, coefficient, precision=precise)
            summed = summed.at[row_ids.reshape(-1)].add(block_output.reshape(-1, CL))
            return summed, None

        far_part, _ = lax.scan(owner_step, jnp.zeros((CLUSTERS, CL), jnp.float32),
                               (col_cluster, row_cluster, ranks, col_factor, row_factor))
        return (near_part + far_part).reshape(-1)

    rate_one, state_one = fault_rates(log_rate, log_state, traction_of(log_rate), load, a_sigma, b_sigma, log_dc)
    mid_rate = log_rate + time_step * rate_one
    mid_state = log_state + time_step * state_one
    rate_two, state_two = fault_rates(mid_rate, mid_state, traction_of(mid_rate), load, a_sigma, b_sigma, log_dc)
    new_log_rate = log_rate + 0.5 * time_step * (rate_one + rate_two)
    new_log_state = log_state + 0.5 * time_step * (state_one + state_two)
    return new_log_rate, new_log_state
```

```python
import functools

import jax
import jax.numpy as jnp
from jax import lax
from jax.experimental import pallas as pl
from jax.experimental.pallas import tpu as pltpu
from jax.sharding import PartitionSpec as P

damping = 0.5
time_step = 0.25
precise = lax.Precision.HIGHEST


def swap_cores(x):
    return lax.ppermute(x, "sub", [(0, 1), (1, 0)])


def swap_owners(x, bit):
    owners = lax.axis_size("blk")
    pairs = [(2 * c + s, 2 * (c ^ bit) + 1 - s) for c in range(owners) for s in range(2)]
    return lax.ppermute(x, ("blk", "sub"), pairs)


def run_copies(pairs, sems):
    copies = [pltpu.make_async_copy(source, target, sems.at[i]) for i, (source, target) in enumerate(pairs)]
    for copy in copies:
        copy.start()
    for copy in copies:
        copy.wait()


def pieces_of(source, target):
    count = source.shape[0]
    parts = next(n for n in (8, 4, 2, 1) if count % n == 0)
    step = count // parts
    return [(source.at[pl.ds(i * step, step)], target.at[pl.ds(i * step, step)]) for i in range(parts)]


def columns_kernel(source, own, target, own_copy, flags, sems):
    run_copies(pieces_of(source, target) + [(own, own_copy)], sems)
    bit = lax.broadcasted_iota(jnp.int32, flags.shape, 0)
    flags[...] = lax.shift_right_logical(lax.axis_index("blk"), bit) & 1


def rows_kernel(source, own, target, own_copy, sems):
    run_copies(pieces_of(source, target), sems)
    own_copy[...] = own[...]


def table_kernel(
    columns_all, rows_all, ranks, near_source, log_rate, log_state, load, a_sigma, b_sigma, log_dc, own,
    columns, own_ranks, place, near, a_copy, lift, own_copy,
    rows, log_rate_in, log_state_in, load_in, b_in, dc_in, sems,
):
    device = lax.axis_index("blk")
    run_copies(
        pieces_of(near_source, near)
        + [
            (columns_all.at[device], columns),
            (ranks.at[0], own_ranks),
            (rows_all.at[device], rows),
            (log_rate, log_rate_in),
            (log_state, log_state_in),
            (load, load_in),
            (a_sigma, a_copy),
            (b_sigma, b_in),
            (log_dc, dc_in),
        ],
        sems,
    )
    own_copy[...] = own[...]
    cluster = lax.broadcasted_iota(jnp.int32, place.shape, 0)
    place[...] = jnp.where(cluster == rows[...], 1.0, 0.0)
    log_values = log_rate_in[...]
    state_rate = jnp.exp(-log_state_in[...]) - jnp.exp(log_values - dc_in[...])
    inverse = (a_copy[...] + damping * jnp.exp(log_values)) * (1.0 / time_step)
    lift[...] = b_in[...] * state_rate - load_in[...] - log_values * inverse


def traction_terms(v_ref, near_start, columns, ranks, place, near, column_factor, row_factor, out, terms):
    leaf = out.shape[1]
    blocks, kmax, _ = column_factor.shape
    near_count = near.shape[0]
    sublane = lax.broadcasted_iota(jnp.int32, (8, 1), 0)

    for b in range(blocks):
        v = v_ref[pl.ds(columns[0, b], 1), :]
        rank = ranks[0, b]
        total = None
        for j in range(0, kmax, 8):
            at = pl.ds(j, 8)
            q = jnp.sum(column_factor[b, at, :] * v, axis=1, keepdims=True)
            q = jnp.where(sublane < rank - j, q, 0.0)
            piece = row_factor[b, at, :] * q
            total = piece if total is None else total + piece
        terms[pl.ds(b, 1), :] = jnp.sum(total, axis=0, keepdims=True)
    out[...] = jnp.dot(
        place[...], terms[...], precision=precise, preferred_element_type=jnp.float32
    )

    lanes = lax.broadcasted_iota(jnp.int32, (leaf, leaf), 1)
    down = lax.broadcasted_iota(jnp.int32, (leaf, leaf), 0)
    for c in range(near_count):
        here = pl.ds(near_start + c, 1)
        total = jnp.sum(near[c] * v_ref[here, :], axis=1, keepdims=True)
        out[here, :] += jnp.sum(jnp.where(lanes == down, total, 0.0), axis=0, keepdims=True)


def near_start_of(near):
    return (2 * lax.axis_index("blk") + lax.axis_index("sub")) * near.shape[0]


def first_kernel(columns, ranks, log_rate, lift, place, near, column_factor, row_factor, out, rate, terms):
    rate[...] = jnp.exp(log_rate[...])
    traction_terms(
        rate, near_start_of(near), columns, ranks, place, near, column_factor, row_factor, out, terms
    )
    per_device = lift.shape[0]
    here = pl.ds(per_device * lax.axis_index("blk"), per_device)
    out[here, :] += jnp.where(lax.axis_index("sub") == 0, lift[...], 0.0)


def second_kernel(
    columns, ranks, lifted, rate_one, a_sigma, place, near, column_factor, row_factor, out, own, rate, terms
):
    mid = lifted[...] * (-time_step / (a_sigma[...] + damping * rate_one[...]))
    rate[...] = mid
    per_device = own.shape[0]
    own[...] = rate[pl.ds(per_device * lax.axis_index("blk"), per_device), :]
    rate[...] = jnp.exp(mid)
    traction_terms(
        rate, near_start_of(near), columns, ranks, place, near, column_factor, row_factor, out, terms
    )


def shards(
    log_rate,
    log_state,
    load,
    a_sigma,
    b_sigma,
    log_dc,
    near_field,
    col_cluster,
    row_cluster,
    ranks,
    col_factor,
    row_factor,
):
    owners = lax.axis_size("blk")
    leaf = near_field.shape[1]
    per_device = log_rate.shape[0] // leaf
    clusters = owners * per_device
    blocks = col_factor.shape[2]
    depth = (owners - 1).bit_length()
    per_own = (per_device, leaf)
    log_rate, log_state, load, a_sigma, b_sigma, log_dc = (
        x.reshape(per_own) for x in (log_rate, log_state, load, a_sigma, b_sigma, log_dc)
    )

    def bit_of(axis):
        return 1 << (depth - 1 - axis)

    def set_in(axis):
        return flags[depth - 1 - axis] != 0

    def joined(axis, own, other):
        first, second = jnp.where(set_in(axis), other, own), jnp.where(set_in(axis), own, other)
        return jnp.concatenate([first, second], axis=axis)

    def flat(x):
        return x.reshape(-1, leaf)

    hbm = pl.BlockSpec(memory_space=pltpu.HBM)
    vmem = pl.BlockSpec(memory_space=pltpu.VMEM)
    smem = pl.BlockSpec(memory_space=pltpu.SMEM)
    limits = pltpu.CompilerParams(vmem_limit_bytes=8 << 20)

    def in_vmem(*shape):
        return pltpu.VMEM(shape, jnp.float32)

    def in_smem(*shape):
        return pltpu.SMEM(shape, jnp.int32)

    def in_hbm(x):
        return pltpu.with_memory_space_constraint(x, pltpu.HBM)

    def hold_factor(kernel, factor, own, own_space, more, name):
        return pl.pallas_call(
            kernel,
            out_shape=(in_vmem(*factor.shape), in_vmem(*own.shape)) + more,
            in_specs=[hbm, own_space],
            out_specs=(vmem,) * (2 + len(more)),
            scratch_shapes=[pltpu.SemaphoreType.DMA((9,))],
            compiler_params=limits,
            cost_estimate=pl.CostEstimate(flops=0, bytes_accessed=8 * factor.size, transcendentals=0),
            name=name,
        )(in_hbm(factor), own)

    def hold_tables(own):
        return pl.pallas_call(
            table_kernel,
            out_shape=(
                in_smem(1, blocks),
                in_smem(1, blocks),
                in_vmem(clusters, blocks),
                in_vmem(*near_field.shape),
                in_vmem(*per_own),
                in_vmem(*per_own),
                in_vmem(*own.shape),
            ),
            in_specs=[hbm] * 10 + [vmem],
            out_specs=(smem, smem) + (vmem,) * 5,
            scratch_shapes=[pltpu.VMEM((1, blocks), jnp.int32)]
            + [in_vmem(*per_own)] * 5
            + [pltpu.SemaphoreType.DMA((17,))],
            compiler_params=limits,
            cost_estimate=pl.CostEstimate(flops=0, bytes_accessed=8 << 20, transcendentals=0),
            name="hold_tables",
        )(
            *(
                in_hbm(x)
                for x in (
                    col_cluster, row_cluster, ranks, near_field,
                    log_rate, log_state, load, a_sigma, b_sigma, log_dc,
                )
            ),
            own,
        )

    rates = log_rate
    held = []
    for axis in range(depth):
        other = swap_owners(rates, bit_of(axis))
        if axis == 0:
            flag_shape = pltpu.VMEM((depth,) + per_own, jnp.int32)
            column_factor, rates, flags = hold_factor(
                columns_kernel, col_factor[0, 0], in_hbm(rates), hbm, (flag_shape,), "hold_columns"
            )
        elif axis == 1:
            row_local, rates = hold_factor(rows_kernel, row_factor[0, 0], rates, vmem, (), "hold_rows")
        elif axis == 2:
            columns, own_ranks, place, near, own_a, lift, rates = hold_tables(rates)
        shape = (2,) * axis + (1,) * (depth - axis) + per_own
        rates = flat(joined(axis, rates.reshape(shape), other.reshape(shape)))

    blocks_and_near = (place, near, column_factor, row_local)
    term_scratch = in_vmem(blocks, leaf)
    part, rate_one = pl.pallas_call(
        first_kernel,
        out_shape=(in_vmem(clusters, leaf), in_vmem(clusters, leaf)),
        in_specs=[smem, smem] + [vmem] * 6,
        out_specs=(vmem, vmem),
        scratch_shapes=[term_scratch],
        compiler_params=limits,
        name="section_one",
    )(columns, own_ranks, rates, lift, *blocks_and_near)

    part = part + swap_cores(part)
    all_a = own_a
    for axis in range(depth):
        other = swap_owners(jnp.concatenate([part, all_a], axis=0), bit_of(axis))
        part = part + other[:clusters]
        shape = (2,) * axis + (1,) * (depth - axis) + per_own
        all_a = flat(joined(axis, all_a.reshape(shape), other[clusters:].reshape(shape)))

    part, mid_rate = pl.pallas_call(
        second_kernel,
        out_shape=(in_vmem(clusters, leaf), in_vmem(*per_own)),
        in_specs=[smem, smem] + [vmem] * 7,
        out_specs=(vmem, vmem),
        scratch_shapes=[in_vmem(clusters, leaf), term_scratch],
        compiler_params=limits,
        name="section_two",
    )(columns, own_ranks, part, rate_one, all_a, *blocks_and_near)

    state_one = jnp.exp(-log_state) - jnp.exp(log_rate - log_dc)
    mid_state = log_state + time_step * state_one
    state_two = jnp.exp(-mid_state) - jnp.exp(mid_rate - log_dc)
    gain_two = 0.5 * time_step / (a_sigma + damping * jnp.exp(mid_rate))
    base_two = 0.5 * (log_rate + mid_rate) + gain_two * (load - b_sigma * state_two)
    new_log_state = log_state + 0.5 * time_step * (state_one + state_two)

    part = part.reshape((2,) * depth + per_own)
    for axis in reversed(range(depth)):
        low = lax.slice_in_dim(part, 0, 1, axis=axis)
        high = lax.slice_in_dim(part, 1, 2, axis=axis)
        send = jnp.where(set_in(axis), low, high)
        keep = jnp.where(set_in(axis), high, low)
        part = keep + swap_owners(flat(send), bit_of(axis)).reshape(keep.shape)
    part = part.reshape(per_own)
    part = part + swap_cores(part)
    new_log_rate = base_two - gain_two * part
    return (new_log_rate.reshape(-1), new_log_state.reshape(-1))


def solution(mesh):
    placed = (
        P(("grp", "blk")),
        P(("grp", "blk")),
        P(("grp", "blk")),
        P(("grp", "blk")),
        P(("grp", "blk")),
        P(("grp", "blk")),
        P(("blk", "sub"), None, None),
        P(None, "sub", None),
        P(None, "sub", None),
        P("blk", "sub", None),
        P("blk", "sub", None, None, None),
        P("blk", "sub", None, None, None),
    )
    return jax.shard_map(
        shards,
        mesh=mesh,
        in_specs=placed,
        out_specs=(P(("grp", "blk")), P(("grp", "blk"))),
        check_vma=False,
    )
```

```python
import functools

import jax
import jax.numpy as jnp
from jax import lax
from jax.experimental import pallas as pl
from jax.experimental.pallas import tpu as pltpu
from jax.sharding import PartitionSpec as P

damping = 0.5
time_step = 0.25
precise = lax.Precision.HIGHEST


def swap_cores(x):
    return lax.ppermute(x, "sub", [(0, 1), (1, 0)])


def swap_owners(x, bit):
    owners = lax.axis_size("blk")
    pairs = [(2 * c + s, 2 * (c ^ bit) + 1 - s) for c in range(owners) for s in range(2)]
    return lax.ppermute(x, ("blk", "sub"), pairs)


def run_copies(pairs, sems):
    copies = [pltpu.make_async_copy(source, target, sems.at[i]) for i, (source, target) in enumerate(pairs)]
    for copy in copies:
        copy.start()
    for copy in copies:
        copy.wait()


def pieces_of(source, target, first=0):
    return [(source.at[pl.ds(first, target.shape[0])], target)]


def near_rows(v_ref, near):
    near_count, leaf, _ = near.shape
    lanes = lax.broadcasted_iota(jnp.int32, (leaf, leaf), 1)
    down = lax.broadcasted_iota(jnp.int32, (leaf, leaf), 0)
    row = lax.broadcasted_iota(jnp.int32, v_ref.shape, 0)
    first = lax.axis_index("sub") * near_count
    placed = jnp.zeros(v_ref.shape, jnp.float32)
    for c in range(near_count):
        total = jnp.sum(near[c] * v_ref[pl.ds(first + c, 1), :], axis=1, keepdims=True)
        total = jnp.sum(jnp.where(lanes == down, total, 0.0), axis=0, keepdims=True)
        placed = jnp.where(row == first + c, total, placed)
    return placed


def first_hold_kernel(
    columns_all, rows_all, ranks, near_source, factor, own,
    table, near_one, own_copy, flags, near, held,
    numbers, rate, sems,
):
    device = lax.axis_index("blk")
    run_copies(
        [
            (own, own_copy),
            (near_source, near),
            (columns_all.at[device], numbers.at[0]),
            (rows_all.at[device], numbers.at[1]),
            (ranks.at[0], numbers.at[2]),
        ]
        + pieces_of(factor, held),
        sems,
    )
    rate[...] = jnp.exp(own_copy[...])
    near_one[...] = near_rows(rate, near)
    table[...] = jnp.zeros(table.shape, jnp.float32)
    for i in range(3):
        table[pl.ds(i, 1), pl.ds(0, numbers.shape[2])] = numbers[i].astype(jnp.float32)
    bit = lax.broadcasted_iota(jnp.int32, flags.shape, 0)
    flags[...] = lax.shift_right_logical(device, bit) & 1


def second_hold_kernel(given, columns, rows, own, held_columns, held_rows, own_copy, sems):
    done = columns.shape[0] - held_columns.shape[0]
    run_copies(pieces_of(columns, held_columns, done) + pieces_of(rows, held_rows), sems)
    own_copy[...] = own[...]


def third_hold_kernel(
    done, given, given_other, factor, log_rate, log_state, load, a_sigma, b_sigma, log_dc, own,
    tables, place, held, a_copy, lift, own_copy,
    log_rate_in, log_state_in, load_in, b_in, dc_in, sems,
):
    run_copies(
        pieces_of(factor, held, done)
        + [
            (given.at[0], tables.at[0]),
            (given_other.at[0], tables.at[1]),
            (log_rate, log_rate_in),
            (log_state, log_state_in),
            (load, load_in),
            (a_sigma, a_copy),
            (b_sigma, b_in),
            (log_dc, dc_in),
        ],
        sems,
    )
    own_copy[...] = own[...]
    blocks = place.shape[2]
    cluster = lax.broadcasted_iota(jnp.int32, place.shape[1:], 0).astype(jnp.float32)
    for g, pack in enumerate((given, given_other)):
        place[g] = jnp.where(cluster == pack[0, 1:2, :blocks], 1.0, 0.0).astype(place.dtype)
    log_values = log_rate_in[...]
    state_rate = jnp.exp(-log_state_in[...]) - jnp.exp(log_values - dc_in[...])
    inverse = (a_copy[...] + damping * jnp.exp(log_values)) * (1.0 / time_step)
    lift[...] = (given[1] + given_other[1]) + (b_in[...] * state_rate - load_in[...] - log_values * inverse)


def near_kernel(mid_rate, near, out, rate):
    rate[...] = jnp.exp(mid_rate[...])
    out[...] = near_rows(rate, near)


def split_three(x):
    parts = []
    for _ in range(3):
        parts.append(x.astype(jnp.bfloat16))
        x = x - parts[-1].astype(jnp.float32)
    return parts


def section(v_ref, tables, known, out, terms):
    place, columns_a, columns_b, rows_a, rows_b, columns_other, rows_other = known
    sublane = lax.broadcasted_iota(jnp.int32, (8, 1), 0)
    summed = None
    for g, column_parts, row_parts in (
        (0, [columns_a, columns_b], [rows_a, rows_b]),
        (1, [columns_other], [rows_other]),
    ):
        column_tiles = [(part, i) for part in column_parts for i in range(part.shape[0])]
        row_tiles = [(part, i) for part in row_parts for i in range(part.shape[0])]
        for b, ((column_factor, i), (row_factor, k)) in enumerate(zip(column_tiles, row_tiles)):
            v = v_ref[pl.ds(tables[g, 0, b].astype(jnp.int32), 1), :]
            rank = tables[g, 2, b].astype(jnp.int32)
            total = None
            for j in range(0, column_factor.shape[1], 8):
                at = pl.ds(j, 8)
                q = jnp.sum(column_factor[i, at, :] * v, axis=1, keepdims=True)
                q = jnp.where(sublane < rank - j, q, 0.0)
                piece = row_factor[k, at, :] * q
                total = piece if total is None else total + piece
            terms[g, pl.ds(b, 1), :] = jnp.sum(total, axis=0, keepdims=True)
        high, middle, low = (
            jnp.dot(place[g], x, preferred_element_type=jnp.float32) for x in split_three(terms[g])
        )
        part = high + (middle + low)
        summed = part if summed is None else summed + part
    out[...] = summed


def first_kernel(tables, log_rate, lift, *refs):
    *known, out, rate, terms = refs
    rate[...] = jnp.exp(log_rate[...])
    section(rate, tables, known, out, terms)
    per_device = lift.shape[0]
    out[pl.ds(per_device * lax.axis_index("blk"), per_device), :] += lift[...]


def second_kernel(tables, lifted, rate_one, a_sigma, *refs):
    *known, out, own, rate, terms = refs
    mid = lifted[...] * (-time_step / (a_sigma[...] + damping * rate_one[...]))
    rate[...] = mid
    per_device = own.shape[0]
    own[...] = rate[pl.ds(per_device * lax.axis_index("blk"), per_device), :]
    rate[...] = jnp.exp(mid)
    section(rate, tables, known, out, terms)


def shards(
    log_rate,
    log_state,
    load,
    a_sigma,
    b_sigma,
    log_dc,
    near_field,
    col_cluster,
    row_cluster,
    ranks,
    col_factor,
    row_factor,
):
    owners = lax.axis_size("blk")
    leaf = near_field.shape[1]
    per_device = log_rate.shape[0] // leaf
    clusters = owners * per_device
    _, _, blocks, kmax, _ = col_factor.shape
    depth = (owners - 1).bit_length()
    per_own = (per_device, leaf)
    log_rate, log_state, load, a_sigma, b_sigma, log_dc = (
        x.reshape(per_own) for x in (log_rate, log_state, load, a_sigma, b_sigma, log_dc)
    )
    col_factor, row_factor = col_factor[0, 0], row_factor[0, 0]

    def bit_of(axis):
        return 1 << (depth - 1 - axis)

    def set_in(axis):
        return flags[depth - 1 - axis] != 0

    def joined(axis, own, other):
        first, second = jnp.where(set_in(axis), other, own), jnp.where(set_in(axis), own, other)
        return jnp.concatenate([first, second], axis=axis)

    def flat(x):
        return x.reshape(-1, leaf)

    hbm = pl.BlockSpec(memory_space=pltpu.HBM)
    vmem = pl.BlockSpec(memory_space=pltpu.VMEM)
    smem = pl.BlockSpec(memory_space=pltpu.SMEM)
    limits = pltpu.CompilerParams(vmem_limit_bytes=8 << 20)

    def in_vmem(*shape):
        return pltpu.VMEM(shape, jnp.float32)

    def in_smem(*shape):
        return pltpu.SMEM(shape, jnp.float32)

    def in_hbm(x):
        return pltpu.with_memory_space_constraint(x, pltpu.HBM)

    def to_vmem(x):
        return pltpu.with_memory_space_constraint(x, pltpu.VMEM)

    def sems(count):
        return pltpu.SemaphoreType.DMA((count,))

    def hold(kernel, name, out_shape, hbm_args, vmem_args, scratch):
        out_space = [smem if x.memory_space == pltpu.SMEM else vmem for x in out_shape]
        return pl.pallas_call(
            kernel,
            out_shape=tuple(out_shape),
            in_specs=[vmem] * len(vmem_args[:-1]) + [hbm] * len(hbm_args) + [vmem] * len(vmem_args[-1:]),
            out_specs=tuple(out_space),
            scratch_shapes=scratch,
            compiler_params=limits,
            cost_estimate=pl.CostEstimate(flops=0, bytes_accessed=4 << 20, transcendentals=0),
            name=name,
        )(*vmem_args[:-1], *(in_hbm(x) for x in hbm_args), *vmem_args[-1:])

    columns_a = blocks // 11 * 6
    rows_a = blocks // 11 * 3

    def factor_part(count):
        return in_vmem(count, kmax, leaf)

    column_other = to_vmem(swap_cores(col_factor))
    row_other = to_vmem(swap_cores(row_factor))

    rates = log_rate
    for axis in range(depth):
        other = swap_owners(rates, bit_of(axis))
        if axis == 0:
            table, near_one, rates, flags, near, part_a = hold(
                first_hold_kernel,
                "hold_first",
                [
                    in_vmem(*per_own),
                    in_vmem(*per_own),
                    in_vmem(*per_own),
                    pltpu.VMEM((depth,) + per_own, jnp.int32),
                    in_vmem(*near_field.shape),
                    factor_part(columns_a),
                ],
                [col_cluster, row_cluster, ranks, near_field, col_factor, rates],
                [],
                [pltpu.VMEM((3, 1, blocks), jnp.int32), in_vmem(*per_own), sems(6)],
            )
            given = jnp.stack([table, near_one])
            given_other = swap_cores(given)
        elif axis == 1:
            part_b, part_c, rates = hold(
                second_hold_kernel,
                "hold_second",
                [factor_part(blocks - columns_a), factor_part(rows_a), in_vmem(*rates.shape)],
                [col_factor, row_factor],
                [given_other, rates],
                [sems(2)],
            )
        elif axis == 2:
            tables, place, part_d, own_a, lift, rates = hold(
                functools.partial(third_hold_kernel, rows_a),
                "hold_third",
                [
                    in_smem(2, *per_own),
                    pltpu.VMEM((2, clusters, blocks), jnp.bfloat16),
                    factor_part(blocks - rows_a),
                    in_vmem(*per_own),
                    in_vmem(*per_own),
                    in_vmem(*rates.shape),
                ],
                [row_factor, log_rate, log_state, load, a_sigma, b_sigma, log_dc],
                [given, given_other, rates],
                [in_vmem(*per_own)] * 5 + [sems(9)],
            )
        shape = (2,) * axis + (1,) * (depth - axis) + per_own
        rates = flat(joined(axis, rates.reshape(shape), other.reshape(shape)))

    known = (place, part_a, part_b, part_c, part_d, column_other, row_other)
    term_scratch = in_vmem(2, blocks, leaf)
    part, rate_one = pl.pallas_call(
        first_kernel,
        out_shape=(in_vmem(clusters, leaf), in_vmem(clusters, leaf)),
        in_specs=[smem] + [vmem] * 9,
        out_specs=(vmem, vmem),
        scratch_shapes=[term_scratch],
        compiler_params=limits,
        name="section_one",
    )(tables, rates, lift, *known)

    all_a = own_a
    for axis in range(depth):
        other = swap_owners(jnp.concatenate([part, all_a], axis=0), bit_of(axis))
        part = part + other[:clusters]
        shape = (2,) * axis + (1,) * (depth - axis) + per_own
        all_a = flat(joined(axis, all_a.reshape(shape), other[clusters:].reshape(shape)))

    part, mid_rate = pl.pallas_call(
        second_kernel,
        out_shape=(in_vmem(clusters, leaf), in_vmem(*per_own)),
        in_specs=[smem] + [vmem] * 10,
        out_specs=(vmem, vmem),
        scratch_shapes=[in_vmem(clusters, leaf), term_scratch],
        compiler_params=limits,
        name="section_two",
    )(tables, part, rate_one, all_a, *known)

    near_two = pl.pallas_call(
        near_kernel,
        out_shape=in_vmem(*per_own),
        in_specs=[vmem, vmem],
        out_specs=vmem,
        scratch_shapes=[in_vmem(*per_own)],
        compiler_params=limits,
        name="near_two",
    )(mid_rate, near)
    near_two = near_two + swap_cores(near_two)

    state_one = jnp.exp(-log_state) - jnp.exp(log_rate - log_dc)
    mid_state = log_state + time_step * state_one
    state_two = jnp.exp(-mid_state) - jnp.exp(mid_rate - log_dc)
    gain_two = 0.5 * time_step / (a_sigma + damping * jnp.exp(mid_rate))
    base_two = 0.5 * (log_rate + mid_rate) + gain_two * (load - b_sigma * state_two)
    new_log_state = log_state + 0.5 * time_step * (state_one + state_two)

    part = part.reshape((2,) * depth + per_own)
    for axis in reversed(range(depth)):
        low = lax.slice_in_dim(part, 0, 1, axis=axis)
        high = lax.slice_in_dim(part, 1, 2, axis=axis)
        send = jnp.where(set_in(axis), low, high)
        keep = jnp.where(set_in(axis), high, low)
        part = keep + swap_owners(flat(send), bit_of(axis)).reshape(keep.shape)
    new_log_rate = base_two - gain_two * (part.reshape(per_own) + near_two)
    return (new_log_rate.reshape(-1), new_log_state.reshape(-1))


def solution(mesh):
    placed = (
        P(("grp", "blk")),
        P(("grp", "blk")),
        P(("grp", "blk")),
        P(("grp", "blk")),
        P(("grp", "blk")),
        P(("grp", "blk")),
        P(("blk", "sub"), None, None),
        P(None, "sub", None),
        P(None, "sub", None),
        P("blk", "sub", None),
        P("blk", "sub", None, None, None),
        P("blk", "sub", None, None, None),
    )
    return jax.shard_map(
        shards,
        mesh=mesh,
        in_specs=placed,
        out_specs=(P(("grp", "blk")), P(("grp", "blk"))),
        check_vma=False,
    )
```

```python
import functools

import jax
import jax.numpy as jnp
from jax import lax
from jax.experimental import pallas as pl
from jax.experimental.pallas import tpu as pltpu
from jax.sharding import PartitionSpec as P

damping = 0.5
time_step = 0.25
precise = lax.Precision.HIGHEST


def swap_cores(x):
    return lax.ppermute(x, "sub", [(0, 1), (1, 0)])


def swap_owners(x, bit, odd_bit=None):
    owners = lax.axis_size("blk")
    bits = (bit, bit if odd_bit is None else odd_bit)
    pairs = [
        (2 * c + s, 2 * (c ^ bits[(c.bit_count() + s) % 2]) + 1 - s) for c in range(owners) for s in range(2)
    ]
    return lax.ppermute(x, ("blk", "sub"), pairs)


def run_copies(pairs, sems):
    copies = [pltpu.make_async_copy(source, target, sems.at[i]) for i, (source, target) in enumerate(pairs)]
    for copy in copies:
        copy.start()
    for copy in copies:
        copy.wait()


def pieces_of(source, target, first=0):
    return [(source.at[pl.ds(first, target.shape[0])], target)]


def near_rows(v_ref, near):
    near_count, leaf, _ = near.shape
    lanes = lax.broadcasted_iota(jnp.int32, (leaf, leaf), 1)
    down = lax.broadcasted_iota(jnp.int32, (leaf, leaf), 0)
    row = lax.broadcasted_iota(jnp.int32, v_ref.shape, 0)
    first = lax.axis_index("sub") * near_count
    placed = jnp.zeros(v_ref.shape, jnp.float32)
    for c in range(near_count):
        total = jnp.sum(near[c] * v_ref[pl.ds(first + c, 1), :], axis=1, keepdims=True)
        total = jnp.sum(jnp.where(lanes == down, total, 0.0), axis=0, keepdims=True)
        placed = jnp.where(row == first + c, total, placed)
    return placed


def first_hold_kernel(
    columns_all, rows_all, ranks, near_source, factor, own,
    table, near_one, own_copy, flags, near, held,
    numbers, rate, sems,
):
    device = lax.axis_index("blk")
    run_copies(
        [
            (own, own_copy),
            (near_source, near),
            (columns_all.at[device], numbers.at[0]),
            (rows_all.at[device], numbers.at[1]),
            (ranks.at[0], numbers.at[2]),
        ]
        + pieces_of(factor, held),
        sems,
    )
    rate[...] = jnp.exp(own_copy[...])
    near_one[...] = near_rows(rate, near)
    table[...] = jnp.zeros(table.shape, jnp.float32)
    for i in range(3):
        table[pl.ds(i, 1), pl.ds(0, numbers.shape[2])] = numbers[i].astype(jnp.float32)
    parity = lax.axis_index("sub")
    for i in range(flags.shape[0] - 1):
        bit = lax.shift_right_logical(device, i) & 1
        parity = parity + bit
        flags[i] = jnp.full(flags.shape[1:], bit, jnp.int32)
    flags[flags.shape[0] - 1] = jnp.full(flags.shape[1:], parity & 1, jnp.int32)


def second_hold_kernel(columns, rows, own, held_columns, held_rows, own_copy, sems):
    done = columns.shape[0] - held_columns.shape[0]
    run_copies(pieces_of(columns, held_columns, done) + pieces_of(rows, held_rows), sems)
    own_copy[...] = own[...]


def third_hold_kernel(
    done, given, given_other, factor, log_rate, log_state, load, a_sigma, b_sigma, log_dc, own,
    tables, place, held, a_copy, lift, own_copy,
    log_rate_in, log_state_in, load_in, b_in, dc_in, sems,
):
    run_copies(
        pieces_of(factor, held, done)
        + [
            (given.at[0], tables.at[0]),
            (given_other.at[0], tables.at[1]),
            (log_rate, log_rate_in),
            (log_state, log_state_in),
            (load, load_in),
            (a_sigma, a_copy),
            (b_sigma, b_in),
            (log_dc, dc_in),
        ],
        sems,
    )
    own_copy[...] = own[...]
    blocks = place.shape[2]
    cluster = lax.broadcasted_iota(jnp.int32, place.shape[1:], 0).astype(jnp.float32)
    for g, pack in enumerate((given, given_other)):
        place[g] = jnp.where(cluster == pack[0, 1:2, :blocks], 1.0, 0.0).astype(place.dtype)
    log_values = log_rate_in[...]
    state_rate = jnp.exp(-log_state_in[...]) - jnp.exp(log_values - dc_in[...])
    inverse = (a_copy[...] + damping * jnp.exp(log_values)) * (1.0 / time_step)
    lift[...] = (given[1] + given_other[1]) + (b_in[...] * state_rate - load_in[...] - log_values * inverse)


def near_kernel(mid_rate, near, out, rate):
    rate[...] = jnp.exp(mid_rate[...])
    out[...] = near_rows(rate, near)


def split_three(x):
    parts = []
    for _ in range(3):
        parts.append(x.astype(jnp.bfloat16))
        x = x - parts[-1].astype(jnp.float32)
    return parts


def section(v_ref, tables, known, out, terms):
    place, columns_a, columns_b, rows_a, rows_b, columns_other, rows_other = known
    sublane = lax.broadcasted_iota(jnp.int32, (8, 1), 0)
    summed = None
    for g, column_parts, row_parts in (
        (0, [columns_a, columns_b], [rows_a, rows_b]),
        (1, [columns_other], [rows_other]),
    ):
        column_tiles = [(part, i) for part in column_parts for i in range(part.shape[0])]
        row_tiles = [(part, i) for part in row_parts for i in range(part.shape[0])]
        for b, ((column_factor, i), (row_factor, k)) in enumerate(zip(column_tiles, row_tiles)):
            v = v_ref[pl.ds(tables[g, 0, b].astype(jnp.int32), 1), :]
            rank = tables[g, 2, b].astype(jnp.int32)
            total = None
            for j in range(0, column_factor.shape[1], 8):
                at = pl.ds(j, 8)
                q = jnp.sum(column_factor[i, at, :] * v, axis=1, keepdims=True)
                q = jnp.where(sublane < rank - j, q, 0.0)
                piece = row_factor[k, at, :] * q
                total = piece if total is None else total + piece
            terms[g, pl.ds(b, 1), :] = jnp.sum(total, axis=0, keepdims=True)
        high, middle, low = (
            jnp.dot(place[g], x, preferred_element_type=jnp.float32) for x in split_three(terms[g])
        )
        part = high + (middle + low)
        summed = part if summed is None else summed + part
    out[...] = summed


def first_kernel(tables, log_rate, lift, *refs):
    *known, out, rate, terms = refs
    rate[...] = jnp.exp(log_rate[...])
    section(rate, tables, known, out, terms)
    per_device = lift.shape[0]
    out[pl.ds(per_device * lax.axis_index("blk"), per_device), :] += lift[...]


def second_kernel(tables, lifted, rate_one, a_sigma, *refs):
    *known, out, own, rate, terms = refs
    mid = lifted[...] * (-time_step / (a_sigma[...] + damping * rate_one[...]))
    rate[...] = mid
    per_device = own.shape[0]
    own[...] = rate[pl.ds(per_device * lax.axis_index("blk"), per_device), :]
    rate[...] = jnp.exp(mid)
    section(rate, tables, known, out, terms)


def shards(
    log_rate,
    log_state,
    load,
    a_sigma,
    b_sigma,
    log_dc,
    near_field,
    col_cluster,
    row_cluster,
    ranks,
    col_factor,
    row_factor,
):
    owners = lax.axis_size("blk")
    leaf = near_field.shape[1]
    per_device = log_rate.shape[0] // leaf
    clusters = owners * per_device
    _, _, blocks, kmax, _ = col_factor.shape
    depth = (owners - 1).bit_length()
    per_own = (per_device, leaf)
    log_rate, log_state, load, a_sigma, b_sigma, log_dc = (
        x.reshape(per_own) for x in (log_rate, log_state, load, a_sigma, b_sigma, log_dc)
    )
    col_factor, row_factor = col_factor[0, 0], row_factor[0, 0]

    def bit_of(axis):
        return 1 << (depth - 1 - axis)

    def set_in(axis):
        return flags[depth - 1 - axis] != 0

    def joined(flag, axis, own, other):
        return jnp.concatenate([jnp.where(flag, other, own), jnp.where(flag, own, other)], axis=axis)

    even_axes = list(range(depth))
    odd_axes = even_axes[::-1]

    def by_kind(even, odd):
        return jnp.where(flags[depth] != 0, odd, even)

    def set_at(step):
        return by_kind(flags[depth - 1 - even_axes[step]], flags[depth - 1 - odd_axes[step]]) != 0

    def hop(x, step):
        return swap_owners(x, bit_of(even_axes[step]), bit_of(odd_axes[step]))

    def rest(axes):
        return list(axes) + [depth, depth + 1]

    def flat(x):
        return x.reshape(-1, leaf)

    hbm = pl.BlockSpec(memory_space=pltpu.HBM)
    vmem = pl.BlockSpec(memory_space=pltpu.VMEM)
    smem = pl.BlockSpec(memory_space=pltpu.SMEM)
    limits = pltpu.CompilerParams(vmem_limit_bytes=8 << 20)

    def in_vmem(*shape):
        return pltpu.VMEM(shape, jnp.float32)

    def in_smem(*shape):
        return pltpu.SMEM(shape, jnp.float32)

    def in_hbm(x):
        return pltpu.with_memory_space_constraint(x, pltpu.HBM)

    def to_vmem(x):
        return pltpu.with_memory_space_constraint(x, pltpu.VMEM)

    def sems(count):
        return pltpu.SemaphoreType.DMA((count,))

    def hold(kernel, name, out_shape, hbm_args, vmem_args, scratch):
        out_space = [smem if x.memory_space == pltpu.SMEM else vmem for x in out_shape]
        return pl.pallas_call(
            kernel,
            out_shape=tuple(out_shape),
            in_specs=[vmem] * len(vmem_args[:-1]) + [hbm] * len(hbm_args) + [vmem] * len(vmem_args[-1:]),
            out_specs=tuple(out_space),
            scratch_shapes=scratch,
            compiler_params=limits,
            cost_estimate=pl.CostEstimate(flops=0, bytes_accessed=4 << 20, transcendentals=0),
            name=name,
        )(*vmem_args[:-1], *(in_hbm(x) for x in hbm_args), *vmem_args[-1:])

    columns_a = blocks // 11 * 4
    rows_a = blocks // 11 * 3

    def factor_part(count):
        return in_vmem(count, kmax, leaf)

    column_other = to_vmem(swap_cores(col_factor))
    row_other = to_vmem(swap_cores(row_factor))

    rates = log_rate
    for axis in range(depth):
        other = swap_owners(rates, bit_of(axis))
        if axis == 0:
            table, near_one, rates, flags, near, part_a = hold(
                first_hold_kernel,
                "hold_first",
                [
                    in_vmem(*per_own),
                    in_vmem(*per_own),
                    in_vmem(*per_own),
                    pltpu.VMEM((depth + 1,) + per_own, jnp.int32),
                    in_vmem(*near_field.shape),
                    factor_part(columns_a),
                ],
                [col_cluster, row_cluster, ranks, near_field, col_factor, rates],
                [],
                [pltpu.VMEM((3, 1, blocks), jnp.int32), in_vmem(*per_own), sems(6)],
            )
            given = jnp.concatenate([jnp.stack([table, near_one]), flags.astype(jnp.float32)], axis=0)
            given_other = swap_cores(given)
        elif axis == 1:
            part_b, part_c, rates = hold(
                second_hold_kernel,
                "hold_second",
                [factor_part(blocks - columns_a), factor_part(rows_a), in_vmem(*rates.shape)],
                [col_factor, row_factor],
                [rates],
                [sems(2)],
            )
        elif axis == 2:
            tables, place, part_d, own_a, lift, rates = hold(
                functools.partial(third_hold_kernel, rows_a),
                "hold_third",
                [
                    in_smem(2, *per_own),
                    pltpu.VMEM((2, clusters, blocks), jnp.bfloat16),
                    factor_part(blocks - rows_a),
                    in_vmem(*per_own),
                    in_vmem(*per_own),
                    in_vmem(*rates.shape),
                ],
                [row_factor, log_rate, log_state, load, a_sigma, b_sigma, log_dc],
                [given, given_other, rates],
                [in_vmem(*per_own)] * 5 + [sems(9)],
            )
        shape = (2,) * axis + (1,) * (depth - axis) + per_own
        flag = given_other[2 + depth - 1 - axis] != 0 if axis == 1 else set_in(axis)
        rates = flat(joined(flag, axis, rates.reshape(shape), other.reshape(shape)))

    known = (place, part_a, part_b, part_c, part_d, column_other, row_other)
    term_scratch = in_vmem(2, blocks, leaf)
    part, rate_one = pl.pallas_call(
        first_kernel,
        out_shape=(in_vmem(clusters, leaf), in_vmem(clusters, leaf)),
        in_specs=[smem] + [vmem] * 9,
        out_specs=(vmem, vmem),
        scratch_shapes=[term_scratch],
        compiler_params=limits,
        name="section_one",
    )(tables, rates, lift, *known)

    all_a = own_a[None]
    for step in range(depth):
        other = hop(jnp.concatenate([part, flat(all_a)], axis=0), step)
        part = part + other[:clusters]
        all_a = joined(set_at(step), 0, all_a, other[clusters:].reshape(all_a.shape))
    all_a = all_a.reshape((2,) * depth + per_own)
    all_a = by_kind(
        *(
            jnp.transpose(all_a, rest(axes[::-1].index(axis) for axis in range(depth)))
            for axes in (even_axes, odd_axes)
        )
    )
    all_a = flat(all_a)

    part, mid_rate = pl.pallas_call(
        second_kernel,
        out_shape=(in_vmem(clusters, leaf), in_vmem(*per_own)),
        in_specs=[smem] + [vmem] * 10,
        out_specs=(vmem, vmem),
        scratch_shapes=[in_vmem(clusters, leaf), term_scratch],
        compiler_params=limits,
        name="section_two",
    )(tables, part, rate_one, all_a, *known)

    near_two = pl.pallas_call(
        near_kernel,
        out_shape=in_vmem(*per_own),
        in_specs=[vmem, vmem],
        out_specs=vmem,
        scratch_shapes=[in_vmem(*per_own)],
        compiler_params=limits,
        name="near_two",
    )(mid_rate, near)
    near_two = near_two + swap_cores(near_two)

    state_one = jnp.exp(-log_state) - jnp.exp(log_rate - log_dc)
    mid_state = log_state + time_step * state_one
    state_two = jnp.exp(-mid_state) - jnp.exp(mid_rate - log_dc)
    gain_two = 0.5 * time_step / (a_sigma + damping * jnp.exp(mid_rate))
    base_two = 0.5 * (log_rate + mid_rate) + gain_two * (load - b_sigma * state_two)
    new_log_state = log_state + 0.5 * time_step * (state_one + state_two)

    part = part.reshape((2,) * depth + per_own)
    for axis in range(depth):
        low = lax.slice_in_dim(part, 0, 1, axis=axis)
        high = lax.slice_in_dim(part, 1, 2, axis=axis)
        send = jnp.where(set_in(axis), low, high)
        keep = jnp.where(set_in(axis), high, low)
        part = keep + swap_owners(flat(send), bit_of(axis)).reshape(keep.shape)
    new_log_rate = base_two - gain_two * (part.reshape(per_own) + near_two)
    return (new_log_rate.reshape(-1), new_log_state.reshape(-1))


def solution(mesh):
    placed = (
        P(("grp", "blk")),
        P(("grp", "blk")),
        P(("grp", "blk")),
        P(("grp", "blk")),
        P(("grp", "blk")),
        P(("grp", "blk")),
        P(("blk", "sub"), None, None),
        P(None, "sub", None),
        P(None, "sub", None),
        P("blk", "sub", None),
        P("blk", "sub", None, None, None),
        P("blk", "sub", None, None, None),
    )
    return jax.shard_map(
        shards,
        mesh=mesh,
        in_specs=placed,
        out_specs=(P(("grp", "blk")), P(("grp", "blk"))),
        check_vma=False,
    )
```

```python
import functools

import jax
import jax.numpy as jnp
from jax import lax
from jax.experimental import pallas as pl
from jax.experimental.pallas import tpu as pltpu
from jax.sharding import PartitionSpec as P

damping = 0.5
time_step = 0.25
precise = lax.Precision.HIGHEST


def swap_cores(x):
    return lax.ppermute(x, "sub", [(0, 1), (1, 0)])


def swap_owners(x, bit, odd_bit=None):
    owners = lax.axis_size("blk")
    bits = (bit, bit if odd_bit is None else odd_bit)
    pairs = [
        (2 * c + s, 2 * (c ^ bits[(c.bit_count() + s) % 2]) + 1 - s) for c in range(owners) for s in range(2)
    ]
    return lax.ppermute(x, ("blk", "sub"), pairs)


def run_copies(pairs, sems):
    copies = [pltpu.make_async_copy(source, target, sems.at[i]) for i, (source, target) in enumerate(pairs)]
    for copy in copies:
        copy.start()
    for copy in copies:
        copy.wait()


def pieces_of(source, target, first=0):
    return [(source.at[pl.ds(first, target.shape[0])], target)]


def near_rows(v_ref, near):
    near_count, leaf, _ = near.shape
    lanes = lax.broadcasted_iota(jnp.int32, (leaf, leaf), 1)
    down = lax.broadcasted_iota(jnp.int32, (leaf, leaf), 0)
    row = lax.broadcasted_iota(jnp.int32, v_ref.shape, 0)
    first = lax.axis_index("sub") * near_count
    placed = jnp.zeros(v_ref.shape, jnp.float32)
    for c in range(near_count):
        total = jnp.sum(near[c] * v_ref[pl.ds(first + c, 1), :], axis=1, keepdims=True)
        total = jnp.sum(jnp.where(lanes == down, total, 0.0), axis=0, keepdims=True)
        placed = jnp.where(row == first + c, total, placed)
    return placed


def first_hold_kernel(
    columns_all, rows_all, ranks, near_source, factor, own,
    table, near_one, own_copy, flags, near, held,
    numbers, rate, sems,
):
    device = lax.axis_index("blk")
    run_copies(
        [
            (own, own_copy),
            (near_source, near),
            (columns_all.at[device], numbers.at[0]),
            (rows_all.at[device], numbers.at[1]),
            (ranks.at[0], numbers.at[2]),
        ]
        + pieces_of(factor, held),
        sems,
    )
    rate[...] = jnp.exp(own_copy[...])
    near_one[...] = near_rows(rate, near)
    table[...] = jnp.zeros(table.shape, jnp.float32)
    for i in range(3):
        table[pl.ds(i, 1), pl.ds(0, numbers.shape[2])] = numbers[i].astype(jnp.float32)
    parity = lax.axis_index("sub")
    for i in range(flags.shape[0] - 1):
        bit = lax.shift_right_logical(device, i) & 1
        parity = parity + bit
        flags[i] = jnp.full(flags.shape[1:], bit, jnp.int32)
    flags[flags.shape[0] - 1] = jnp.full(flags.shape[1:], parity & 1, jnp.int32)


def second_hold_kernel(columns, rows, own, held_columns, held_rows, own_copy, sems):
    done = columns.shape[0] - held_columns.shape[0]
    run_copies(pieces_of(columns, held_columns, done) + pieces_of(rows, held_rows), sems)
    own_copy[...] = own[...]


def third_hold_kernel(
    done, given, given_other, factor, log_rate, log_state, load, a_sigma, b_sigma, log_dc, own,
    tables, place, held, a_copy, lift, own_copy,
    log_rate_in, log_state_in, load_in, b_in, dc_in, sems,
):
    run_copies(
        pieces_of(factor, held, done)
        + [
            (given.at[0], tables.at[0]),
            (given_other.at[0], tables.at[1]),
            (log_rate, log_rate_in),
            (log_state, log_state_in),
            (load, load_in),
            (a_sigma, a_copy),
            (b_sigma, b_in),
            (log_dc, dc_in),
        ],
        sems,
    )
    own_copy[...] = own[...]
    blocks = place.shape[2]
    cluster = lax.broadcasted_iota(jnp.int32, place.shape[1:], 0).astype(jnp.float32)
    for g, pack in enumerate((given, given_other)):
        place[g] = jnp.where(cluster == pack[0, 1:2, :blocks], 1.0, 0.0).astype(place.dtype)
    log_values = log_rate_in[...]
    state_rate = jnp.exp(-log_state_in[...]) - jnp.exp(log_values - dc_in[...])
    inverse = (a_copy[...] + damping * jnp.exp(log_values)) * (1.0 / time_step)
    lift[...] = (given[1] + given_other[1]) + (b_in[...] * state_rate - load_in[...] - log_values * inverse)


def finish_kernel(
    mid_rate, log_rate, log_state, load, a_sigma, b_sigma, log_dc, near,
    near_two, base_two, gain_two, new_log_state, rate,
    log_rate_in, log_state_in, load_in, a_in, b_in, dc_in, sems,
):
    run_copies(
        [
            (log_rate, log_rate_in),
            (log_state, log_state_in),
            (load, load_in),
            (a_sigma, a_in),
            (b_sigma, b_in),
            (log_dc, dc_in),
        ],
        sems,
    )
    mid = mid_rate[...]
    rate[...] = jnp.exp(mid)
    near_two[...] = near_rows(rate, near)
    states = log_state_in[...]
    state_one = jnp.exp(-states) - jnp.exp(log_rate_in[...] - dc_in[...])
    state_two = jnp.exp(-(states + time_step * state_one)) - jnp.exp(mid - dc_in[...])
    gain = 0.5 * time_step / (a_in[...] + damping * rate[...])
    gain_two[...] = gain
    base_two[...] = 0.5 * (log_rate_in[...] + mid) + gain * (load_in[...] - b_in[...] * state_two)
    new_log_state[...] = states + 0.5 * time_step * (state_one + state_two)


def split_three(x):
    parts = []
    for _ in range(3):
        parts.append(x.astype(jnp.bfloat16))
        x = x - parts[-1].astype(jnp.float32)
    return parts


def section(v_ref, tables, known, out, terms):
    place, columns_a, columns_b, rows_a, rows_b, columns_other, rows_other = known
    sublane = lax.broadcasted_iota(jnp.int32, (8, 1), 0)
    summed = None
    for g, column_parts, row_parts in (
        (0, [columns_a, columns_b], [rows_a, rows_b]),
        (1, [columns_other], [rows_other]),
    ):
        column_tiles = [(part, i) for part in column_parts for i in range(part.shape[0])]
        row_tiles = [(part, i) for part in row_parts for i in range(part.shape[0])]
        for b, ((column_factor, i), (row_factor, k)) in enumerate(zip(column_tiles, row_tiles)):
            v = v_ref[pl.ds(tables[g, 0, b].astype(jnp.int32), 1), :]
            rank = tables[g, 2, b].astype(jnp.int32)
            total = None
            for j in range(0, column_factor.shape[1], 8):
                at = pl.ds(j, 8)
                q = jnp.sum(column_factor[i, at, :] * v, axis=1, keepdims=True)
                q = jnp.where(sublane < rank - j, q, 0.0)
                piece = row_factor[k, at, :] * q
                total = piece if total is None else total + piece
            terms[g, pl.ds(b, 1), :] = jnp.sum(total, axis=0, keepdims=True)
        high, middle, low = (
            jnp.dot(place[g], x, preferred_element_type=jnp.float32) for x in split_three(terms[g])
        )
        part = high + (middle + low)
        summed = part if summed is None else summed + part
    out[...] = summed


def first_kernel(tables, log_rate, lift, *refs):
    *known, out, rate, terms = refs
    rate[...] = jnp.exp(log_rate[...])
    section(rate, tables, known, out, terms)
    per_device = lift.shape[0]
    out[pl.ds(per_device * lax.axis_index("blk"), per_device), :] += lift[...]


def second_kernel(tables, lifted, rate_one, a_sigma, *refs):
    *known, out, own, rate, terms = refs
    mid = lifted[...] * (-time_step / (a_sigma[...] + damping * rate_one[...]))
    rate[...] = mid
    per_device = own.shape[0]
    own[...] = rate[pl.ds(per_device * lax.axis_index("blk"), per_device), :]
    rate[...] = jnp.exp(mid)
    section(rate, tables, known, out, terms)


def shards(
    log_rate,
    log_state,
    load,
    a_sigma,
    b_sigma,
    log_dc,
    near_field,
    col_cluster,
    row_cluster,
    ranks,
    col_factor,
    row_factor,
):
    owners = lax.axis_size("blk")
    leaf = near_field.shape[1]
    per_device = log_rate.shape[0] // leaf
    clusters = owners * per_device
    _, _, blocks, kmax, _ = col_factor.shape
    depth = (owners - 1).bit_length()
    per_own = (per_device, leaf)
    log_rate, log_state, load, a_sigma, b_sigma, log_dc = (
        x.reshape(per_own) for x in (log_rate, log_state, load, a_sigma, b_sigma, log_dc)
    )
    col_factor, row_factor = col_factor[0, 0], row_factor[0, 0]

    def bit_of(axis):
        return 1 << (depth - 1 - axis)

    def set_in(axis):
        return flags[depth - 1 - axis] != 0

    def joined(flag, axis, own, other):
        return jnp.concatenate([jnp.where(flag, other, own), jnp.where(flag, own, other)], axis=axis)

    even_axes = list(range(depth))
    odd_axes = even_axes[::-1]

    def by_kind(even, odd):
        return jnp.where(flags[depth] != 0, odd, even)

    def set_at(step):
        return by_kind(flags[depth - 1 - even_axes[step]], flags[depth - 1 - odd_axes[step]]) != 0

    def hop(x, step):
        return swap_owners(x, bit_of(even_axes[step]), bit_of(odd_axes[step]))

    def rest(axes):
        return list(axes) + [depth, depth + 1]

    def flat(x):
        return x.reshape(-1, leaf)

    hbm = pl.BlockSpec(memory_space=pltpu.HBM)
    vmem = pl.BlockSpec(memory_space=pltpu.VMEM)
    smem = pl.BlockSpec(memory_space=pltpu.SMEM)
    limits = pltpu.CompilerParams(vmem_limit_bytes=8 << 20)

    def in_vmem(*shape):
        return pltpu.VMEM(shape, jnp.float32)

    def in_smem(*shape):
        return pltpu.SMEM(shape, jnp.float32)

    def in_hbm(x):
        return pltpu.with_memory_space_constraint(x, pltpu.HBM)

    def to_vmem(x):
        return pltpu.with_memory_space_constraint(x, pltpu.VMEM)

    def sems(count):
        return pltpu.SemaphoreType.DMA((count,))

    def hold(kernel, name, out_shape, hbm_args, vmem_args, scratch):
        out_space = [smem if x.memory_space == pltpu.SMEM else vmem for x in out_shape]
        return pl.pallas_call(
            kernel,
            out_shape=tuple(out_shape),
            in_specs=[vmem] * len(vmem_args[:-1]) + [hbm] * len(hbm_args) + [vmem] * len(vmem_args[-1:]),
            out_specs=tuple(out_space),
            scratch_shapes=scratch,
            compiler_params=limits,
            cost_estimate=pl.CostEstimate(flops=0, bytes_accessed=4 << 20, transcendentals=0),
            name=name,
        )(*vmem_args[:-1], *(in_hbm(x) for x in hbm_args), *vmem_args[-1:])

    columns_a = blocks // 11 * 4
    rows_a = blocks // 11 * 3

    def factor_part(count):
        return in_vmem(count, kmax, leaf)

    column_other = to_vmem(swap_cores(col_factor))
    row_other = to_vmem(swap_cores(row_factor))

    rates = log_rate
    for axis in range(depth):
        other = swap_owners(rates, bit_of(axis))
        if axis == 0:
            table, near_one, rates, flags, near, part_a = hold(
                first_hold_kernel,
                "hold_first",
                [
                    in_vmem(*per_own),
                    in_vmem(*per_own),
                    in_vmem(*per_own),
                    pltpu.VMEM((depth + 1,) + per_own, jnp.int32),
                    in_vmem(*near_field.shape),
                    factor_part(columns_a),
                ],
                [col_cluster, row_cluster, ranks, near_field, col_factor, rates],
                [],
                [pltpu.VMEM((3, 1, blocks), jnp.int32), in_vmem(*per_own), sems(6)],
            )
            given = jnp.concatenate([jnp.stack([table, near_one]), flags.astype(jnp.float32)], axis=0)
            given_other = swap_cores(given)
        elif axis == 1:
            part_b, part_c, rates = hold(
                second_hold_kernel,
                "hold_second",
                [factor_part(blocks - columns_a), factor_part(rows_a), in_vmem(*rates.shape)],
                [col_factor, row_factor],
                [rates],
                [sems(2)],
            )
        elif axis == 2:
            tables, place, part_d, own_a, lift, rates = hold(
                functools.partial(third_hold_kernel, rows_a),
                "hold_third",
                [
                    in_smem(2, *per_own),
                    pltpu.VMEM((2, clusters, blocks), jnp.bfloat16),
                    factor_part(blocks - rows_a),
                    in_vmem(*per_own),
                    in_vmem(*per_own),
                    in_vmem(*rates.shape),
                ],
                [row_factor, log_rate, log_state, load, a_sigma, b_sigma, log_dc],
                [given, given_other, rates],
                [in_vmem(*per_own)] * 5 + [sems(9)],
            )
        shape = (2,) * axis + (1,) * (depth - axis) + per_own
        flag = given_other[2 + depth - 1 - axis] != 0 if axis == 1 else set_in(axis)
        rates = flat(joined(flag, axis, rates.reshape(shape), other.reshape(shape)))

    known = (place, part_a, part_b, part_c, part_d, column_other, row_other)
    term_scratch = in_vmem(2, blocks, leaf)
    part, rate_one = pl.pallas_call(
        first_kernel,
        out_shape=(in_vmem(clusters, leaf), in_vmem(clusters, leaf)),
        in_specs=[smem] + [vmem] * 9,
        out_specs=(vmem, vmem),
        scratch_shapes=[term_scratch],
        compiler_params=limits,
        name="section_one",
    )(tables, rates, lift, *known)

    all_a = own_a[None]
    for step in range(depth):
        other = hop(jnp.concatenate([part, flat(all_a)], axis=0), step)
        part = part + other[:clusters]
        all_a = joined(set_at(step), 0, all_a, other[clusters:].reshape(all_a.shape))
    all_a = all_a.reshape((2,) * depth + per_own)
    all_a = by_kind(
        *(
            jnp.transpose(all_a, rest(axes[::-1].index(axis) for axis in range(depth)))
            for axes in (even_axes, odd_axes)
        )
    )
    all_a = flat(all_a)

    part, mid_rate = pl.pallas_call(
        second_kernel,
        out_shape=(in_vmem(clusters, leaf), in_vmem(*per_own)),
        in_specs=[smem] + [vmem] * 10,
        out_specs=(vmem, vmem),
        scratch_shapes=[in_vmem(clusters, leaf), term_scratch],
        compiler_params=limits,
        name="section_two",
    )(tables, part, rate_one, all_a, *known)

    near_two, base_two, gain_two, new_log_state = hold(
        finish_kernel,
        "finish",
        [in_vmem(*per_own)] * 4,
        [log_rate, log_state, load, a_sigma, b_sigma, log_dc],
        [mid_rate, near],
        [in_vmem(*per_own)] * 7 + [sems(6)],
    )
    near_two = near_two + swap_cores(near_two)

    part = part.reshape((2,) * depth + per_own)
    for axis in range(depth):
        low = lax.slice_in_dim(part, 0, 1, axis=axis)
        high = lax.slice_in_dim(part, 1, 2, axis=axis)
        send = jnp.where(set_in(axis), low, high)
        keep = jnp.where(set_in(axis), high, low)
        part = keep + swap_owners(flat(send), bit_of(axis)).reshape(keep.shape)
    new_log_rate = base_two - gain_two * (part.reshape(per_own) + near_two)
    return (new_log_rate.reshape(-1), new_log_state.reshape(-1))


def solution(mesh):
    placed = (
        P(("grp", "blk")),
        P(("grp", "blk")),
        P(("grp", "blk")),
        P(("grp", "blk")),
        P(("grp", "blk")),
        P(("grp", "blk")),
        P(("blk", "sub"), None, None),
        P(None, "sub", None),
        P(None, "sub", None),
        P("blk", "sub", None),
        P("blk", "sub", None, None, None),
        P("blk", "sub", None, None, None),
    )
    return jax.shard_map(
        shards,
        mesh=mesh,
        in_specs=placed,
        out_specs=(P(("grp", "blk")), P(("grp", "blk"))),
        check_vma=False,
    )
```

```python
import functools

import jax
import jax.numpy as jnp
from jax import lax
from jax.experimental import pallas as pl
from jax.experimental.pallas import tpu as pltpu
from jax.sharding import PartitionSpec as P

damping = 0.5
time_step = 0.25
precise = lax.Precision.HIGHEST


def swap_cores(x):
    return lax.ppermute(x, "sub", [(0, 1), (1, 0)])


def swap_owners(x, bit, odd_bit=None):
    owners = lax.axis_size("blk")
    bits = (bit, bit if odd_bit is None else odd_bit)
    pairs = [
        (2 * c + s, 2 * (c ^ bits[(c.bit_count() + s) % 2]) + 1 - s) for c in range(owners) for s in range(2)
    ]
    return lax.ppermute(x, ("blk", "sub"), pairs)


def run_copies(pairs, sems):
    copies = [pltpu.make_async_copy(source, target, sems.at[i]) for i, (source, target) in enumerate(pairs)]
    for copy in copies:
        copy.start()
    for copy in copies:
        copy.wait()


def pieces_of(source, target, first=0):
    return [(source.at[pl.ds(first, target.shape[0])], target)]


def near_rows(v_ref, near):
    near_count, leaf, _ = near.shape
    lanes = lax.broadcasted_iota(jnp.int32, (leaf, leaf), 1)
    down = lax.broadcasted_iota(jnp.int32, (leaf, leaf), 0)
    row = lax.broadcasted_iota(jnp.int32, v_ref.shape, 0)
    first = lax.axis_index("sub") * near_count
    placed = jnp.zeros(v_ref.shape, jnp.float32)
    for c in range(near_count):
        total = jnp.sum(near[c] * v_ref[pl.ds(first + c, 1), :], axis=1, keepdims=True)
        total = jnp.sum(jnp.where(lanes == down, total, 0.0), axis=0, keepdims=True)
        placed = jnp.where(row == first + c, total, placed)
    return placed


def first_hold_kernel(
    columns_all, rows_all, ranks, near_source, factor, own,
    table, near_one, own_copy, flags, near, held,
    numbers, rate, sems,
):
    device = lax.axis_index("blk")
    run_copies(
        [
            (own, own_copy),
            (near_source, near),
            (columns_all.at[device], numbers.at[0]),
            (rows_all.at[device], numbers.at[1]),
            (ranks.at[0], numbers.at[2]),
        ]
        + pieces_of(factor, held),
        sems,
    )
    rate[...] = jnp.exp(own_copy[...])
    near_one[...] = near_rows(rate, near)
    table[...] = jnp.zeros(table.shape, jnp.float32)
    for i in range(3):
        table[pl.ds(i, 1), pl.ds(0, numbers.shape[2])] = numbers[i].astype(jnp.float32)
    parity = lax.axis_index("sub")
    for i in range(flags.shape[0] - 1):
        bit = lax.shift_right_logical(device, i) & 1
        parity = parity + bit
        flags[i] = jnp.full(flags.shape[1:], bit, jnp.int32)
    flags[flags.shape[0] - 1] = jnp.full(flags.shape[1:], parity & 1, jnp.int32)


def second_hold_kernel(columns, rows, own, held_columns, held_rows, own_copy, sems):
    done = columns.shape[0] - held_columns.shape[0]
    run_copies(pieces_of(columns, held_columns, done) + pieces_of(rows, held_rows), sems)
    own_copy[...] = own[...]


def third_hold_kernel(
    done, given, given_other, factor, log_rate, log_state, load, a_sigma, b_sigma, log_dc, own,
    tables, place, held, a_copy, lift, own_copy,
    log_rate_in, log_state_in, load_in, b_in, dc_in, sems,
):
    run_copies(
        pieces_of(factor, held, done)
        + [
            (given.at[0], tables.at[0]),
            (given_other.at[0], tables.at[1]),
            (log_rate, log_rate_in),
            (log_state, log_state_in),
            (load, load_in),
            (a_sigma, a_copy),
            (b_sigma, b_in),
            (log_dc, dc_in),
        ],
        sems,
    )
    own_copy[...] = own[...]
    blocks = place.shape[2]
    cluster = lax.broadcasted_iota(jnp.int32, place.shape[1:], 0).astype(jnp.float32)
    for g, pack in enumerate((given, given_other)):
        place[g] = jnp.where(cluster == pack[0, 1:2, :blocks], 1.0, 0.0).astype(place.dtype)
    log_values = log_rate_in[...]
    state_rate = jnp.exp(-log_state_in[...]) - jnp.exp(log_values - dc_in[...])
    inverse = (a_copy[...] + damping * jnp.exp(log_values)) * (1.0 / time_step)
    lift[...] = (given[1] + given_other[1]) + (b_in[...] * state_rate - load_in[...] - log_values * inverse)


def finish_kernel(
    mid_rate, log_rate, log_state, load, a_sigma, b_sigma, log_dc, near,
    near_two, base_two, gain_two, new_log_state, rate,
    log_rate_in, log_state_in, load_in, a_in, b_in, dc_in, sems,
):
    run_copies(
        [
            (log_rate, log_rate_in),
            (log_state, log_state_in),
            (load, load_in),
            (a_sigma, a_in),
            (b_sigma, b_in),
            (log_dc, dc_in),
        ],
        sems,
    )
    mid = mid_rate[...]
    rate[...] = jnp.exp(mid)
    near_two[...] = near_rows(rate, near)
    states = log_state_in[...]
    state_one = jnp.exp(-states) - jnp.exp(log_rate_in[...] - dc_in[...])
    state_two = jnp.exp(-(states + time_step * state_one)) - jnp.exp(mid - dc_in[...])
    gain = 0.5 * time_step / (a_in[...] + damping * rate[...])
    gain_two[...] = gain
    base_two[...] = 0.5 * (log_rate_in[...] + mid) + gain * (load_in[...] - b_in[...] * state_two)
    new_log_state[...] = states + 0.5 * time_step * (state_one + state_two)


def split_three(x):
    parts = []
    for _ in range(3):
        parts.append(x.astype(jnp.bfloat16))
        x = x - parts[-1].astype(jnp.float32)
    return parts


def section(v_ref, tables, known, out, terms):
    place, columns_a, columns_b, rows_a, rows_b, columns_other, rows_other = known
    sublane = lax.broadcasted_iota(jnp.int32, (8, 1), 0)
    summed = None
    for g, column_parts, row_parts in (
        (0, [columns_a, columns_b], [rows_a, rows_b]),
        (1, [columns_other], [rows_other]),
    ):
        column_tiles = [(part, i) for part in column_parts for i in range(part.shape[0])]
        row_tiles = [(part, i) for part in row_parts for i in range(part.shape[0])]
        for b, ((column_factor, i), (row_factor, k)) in enumerate(zip(column_tiles, row_tiles)):
            v = v_ref[pl.ds(tables[g, 0, b].astype(jnp.int32), 1), :]
            rank = tables[g, 2, b].astype(jnp.int32)
            total = None
            for j in range(0, column_factor.shape[1], 8):
                at = pl.ds(j, 8)
                q = jnp.sum(column_factor[i, at, :] * v, axis=1, keepdims=True)
                q = jnp.where(sublane < rank - j, q, 0.0)
                piece = row_factor[k, at, :] * q
                total = piece if total is None else total + piece
            terms[g, pl.ds(b, 1), :] = jnp.sum(total, axis=0, keepdims=True)
        high, middle, low = (
            jnp.dot(place[g], x, preferred_element_type=jnp.float32) for x in split_three(terms[g])
        )
        part = high + (middle + low)
        summed = part if summed is None else summed + part
    out[...] = summed


def first_kernel(tables, log_rate, lift, *refs):
    *known, out, rate, terms = refs
    rate[...] = jnp.exp(log_rate[...])
    section(rate, tables, known, out, terms)
    per_device = lift.shape[0]
    out[pl.ds(per_device * lax.axis_index("blk"), per_device), :] += lift[...]


def second_kernel(tables, lifted, rate_one, a_sigma, *refs):
    *known, out, own, rate, terms = refs
    mid = lifted[...] * (-time_step / (a_sigma[...] + damping * rate_one[...]))
    rate[...] = mid
    per_device = own.shape[0]
    own[...] = rate[pl.ds(per_device * lax.axis_index("blk"), per_device), :]
    rate[...] = jnp.exp(mid)
    section(rate, tables, known, out, terms)


def shards(
    log_rate,
    log_state,
    load,
    a_sigma,
    b_sigma,
    log_dc,
    near_field,
    col_cluster,
    row_cluster,
    ranks,
    col_factor,
    row_factor,
):
    owners = lax.axis_size("blk")
    leaf = near_field.shape[1]
    per_device = log_rate.shape[0] // leaf
    clusters = owners * per_device
    _, _, blocks, kmax, _ = col_factor.shape
    depth = (owners - 1).bit_length()
    per_own = (per_device, leaf)
    log_rate, log_state, load, a_sigma, b_sigma, log_dc = (
        x.reshape(per_own) for x in (log_rate, log_state, load, a_sigma, b_sigma, log_dc)
    )
    col_factor, row_factor = col_factor[0, 0], row_factor[0, 0]

    def bit_of(axis):
        return 1 << (depth - 1 - axis)

    def set_in(axis):
        return flags[depth - 1 - axis] != 0

    def joined(flag, axis, own, other):
        return jnp.concatenate([jnp.where(flag, other, own), jnp.where(flag, own, other)], axis=axis)

    even_axes = list(range(depth))
    odd_axes = even_axes[::-1]

    def by_kind(even, odd):
        return jnp.where(flags[depth] != 0, odd, even)

    def set_at(axes):
        return by_kind(*(flags[depth - 1 - axis] for axis in axes)) != 0

    def hop(x, axes):
        return swap_owners(x, *(bit_of(axis) for axis in axes))

    def rest(axes):
        return list(axes) + [depth, depth + 1]

    def flat(x):
        return x.reshape(-1, leaf)

    hbm = pl.BlockSpec(memory_space=pltpu.HBM)
    vmem = pl.BlockSpec(memory_space=pltpu.VMEM)
    smem = pl.BlockSpec(memory_space=pltpu.SMEM)
    limits = pltpu.CompilerParams(vmem_limit_bytes=8 << 20)

    def in_vmem(*shape):
        return pltpu.VMEM(shape, jnp.float32)

    def in_smem(*shape):
        return pltpu.SMEM(shape, jnp.float32)

    def in_hbm(x):
        return pltpu.with_memory_space_constraint(x, pltpu.HBM)

    def to_vmem(x):
        return pltpu.with_memory_space_constraint(x, pltpu.VMEM)

    def sems(count):
        return pltpu.SemaphoreType.DMA((count,))

    def hold(kernel, name, out_shape, hbm_args, vmem_args, scratch):
        out_space = [smem if x.memory_space == pltpu.SMEM else vmem for x in out_shape]
        return pl.pallas_call(
            kernel,
            out_shape=tuple(out_shape),
            in_specs=[vmem] * len(vmem_args[:-1]) + [hbm] * len(hbm_args) + [vmem] * len(vmem_args[-1:]),
            out_specs=tuple(out_space),
            scratch_shapes=scratch,
            compiler_params=limits,
            cost_estimate=pl.CostEstimate(flops=0, bytes_accessed=4 << 20, transcendentals=0),
            name=name,
        )(*vmem_args[:-1], *(in_hbm(x) for x in hbm_args), *vmem_args[-1:])

    columns_a = blocks // 11 * 4
    rows_a = blocks // 11 * 4

    def factor_part(count):
        return in_vmem(count, kmax, leaf)

    column_other = to_vmem(swap_cores(col_factor))
    row_other = to_vmem(swap_cores(row_factor))

    rates = log_rate
    for axis in range(depth):
        other = swap_owners(rates, bit_of(axis))
        if axis == 0:
            table, near_one, rates, flags, near, part_a = hold(
                first_hold_kernel,
                "hold_first",
                [
                    in_vmem(*per_own),
                    in_vmem(*per_own),
                    in_vmem(*per_own),
                    pltpu.VMEM((depth + 1,) + per_own, jnp.int32),
                    in_vmem(*near_field.shape),
                    factor_part(columns_a),
                ],
                [col_cluster, row_cluster, ranks, near_field, col_factor, rates],
                [],
                [pltpu.VMEM((3, 1, blocks), jnp.int32), in_vmem(*per_own), sems(6)],
            )
            given = jnp.concatenate([jnp.stack([table, near_one]), flags.astype(jnp.float32)], axis=0)
            given_other = swap_cores(given)
        elif axis == 1:
            part_b, part_c, rates = hold(
                second_hold_kernel,
                "hold_second",
                [factor_part(blocks - columns_a), factor_part(rows_a), in_vmem(*rates.shape)],
                [col_factor, row_factor],
                [rates],
                [sems(2)],
            )
        elif axis == 2:
            tables, place, part_d, own_a, lift, rates = hold(
                functools.partial(third_hold_kernel, rows_a),
                "hold_third",
                [
                    in_smem(2, *per_own),
                    pltpu.VMEM((2, clusters, blocks), jnp.bfloat16),
                    factor_part(blocks - rows_a),
                    in_vmem(*per_own),
                    in_vmem(*per_own),
                    in_vmem(*rates.shape),
                ],
                [row_factor, log_rate, log_state, load, a_sigma, b_sigma, log_dc],
                [given, given_other, rates],
                [in_vmem(*per_own)] * 5 + [sems(9)],
            )
        shape = (2,) * axis + (1,) * (depth - axis) + per_own
        flag = given_other[2 + depth - 1 - axis] != 0 if axis == 1 else set_in(axis)
        rates = flat(joined(flag, axis, rates.reshape(shape), other.reshape(shape)))

    known = (place, part_a, part_b, part_c, part_d, column_other, row_other)
    term_scratch = in_vmem(2, blocks, leaf)
    part, rate_one = pl.pallas_call(
        first_kernel,
        out_shape=(in_vmem(clusters, leaf), in_vmem(clusters, leaf)),
        in_specs=[smem] + [vmem] * 9,
        out_specs=(vmem, vmem),
        scratch_shapes=[term_scratch],
        compiler_params=limits,
        name="section_one",
    )(tables, rates, lift, *known)

    all_a = own_a[None]
    for axes in zip(even_axes, odd_axes):
        other = hop(jnp.concatenate([part, flat(all_a)], axis=0), axes)
        part = part + other[:clusters]
        all_a = joined(set_at(axes), 0, all_a, other[clusters:].reshape(all_a.shape))
    all_a = all_a.reshape((2,) * depth + per_own)
    all_a = by_kind(
        *(
            jnp.transpose(all_a, rest(axes[::-1].index(axis) for axis in range(depth)))
            for axes in (even_axes, odd_axes)
        )
    )
    all_a = flat(all_a)

    part, mid_rate = pl.pallas_call(
        second_kernel,
        out_shape=(in_vmem(clusters, leaf), in_vmem(*per_own)),
        in_specs=[smem] + [vmem] * 10,
        out_specs=(vmem, vmem),
        scratch_shapes=[in_vmem(clusters, leaf), term_scratch],
        compiler_params=limits,
        name="section_two",
    )(tables, part, rate_one, all_a, *known)

    near_two, base_two, gain_two, new_log_state = hold(
        finish_kernel,
        "finish",
        [in_vmem(*per_own)] * 4,
        [log_rate, log_state, load, a_sigma, b_sigma, log_dc],
        [mid_rate, near],
        [in_vmem(*per_own)] * 7 + [sems(6)],
    )
    near_two = near_two + swap_cores(near_two)

    last_even, last_odd = even_axes, even_axes[:1] + even_axes[:0:-1]
    part = part.reshape((2,) * depth + per_own)
    part = by_kind(jnp.transpose(part, rest(last_even)), jnp.transpose(part, rest(last_odd)))
    for axes in zip(last_even, last_odd):
        flag = set_at(axes)
        send, keep = jnp.where(flag, part[0], part[1]), jnp.where(flag, part[1], part[0])
        part = keep + hop(flat(send), axes).reshape(keep.shape)
    new_log_rate = base_two - gain_two * (part.reshape(per_own) + near_two)
    return (new_log_rate.reshape(-1), new_log_state.reshape(-1))


def solution(mesh):
    placed = (
        P(("grp", "blk")),
        P(("grp", "blk")),
        P(("grp", "blk")),
        P(("grp", "blk")),
        P(("grp", "blk")),
        P(("grp", "blk")),
        P(("blk", "sub"), None, None),
        P(None, "sub", None),
        P(None, "sub", None),
        P("blk", "sub", None),
        P("blk", "sub", None, None, None),
        P("blk", "sub", None, None, None),
    )
    return jax.shard_map(
        shards,
        mesh=mesh,
        in_specs=placed,
        out_specs=(P(("grp", "blk")), P(("grp", "blk"))),
        check_vma=False,
    )
```
